512 devices in a mesh: seq: 32 (over x_hi, z, core), exp: 16 (over y, x_lo).
Axes of the slice: x: 4 (x_hi: 2, x_lo: 2; x = x_hi * 2 + x_lo), y: 8, z: 8, core: 2. Of those that a mesh axis runs over, the one named last changes fastest.
Arguments:
- tokens: bfloat16 [262144, 1280], P(('seq', 'exp')), may hold values from -1024 to 1024
- slot_embed: bfloat16 [256, 1280], P('exp', 'seq'), may hold values from -2 to 2
- slot_outputs: bfloat16 [256, 1280], P('exp', 'seq'), may hold values from -6 to 6
- output_grad: bfloat16 [262144, 1280], P(('seq', 'exp')), may hold values from -2560 to 2560
- slot_input_grad: bfloat16 [256, 1280], P('exp', 'seq'), may hold values from -73728 to 73728
Outputs:
- token_grad: bfloat16 [262144, 1280], P(('seq', 'exp'))
- embed_grad: float32 [256, 1280], P('exp', 'seq')
- slot_output_grad: float32 [256, 1280], P('exp', 'seq')
The draws below stay inside these ranges and needn't reach their ends.
All inputs are finite; a program needn't handle non-finite values.
Results may differ from the reference program's by a relative error of at most 0.0051.
Values may be sent and summed in bfloat16 or wider, within the bound.
No kernel may reach another device: no remote copies, remote signals or barrier semaphores. Data moves between devices by JAX's collectives and lax.ppermute only.
A program may use at most 64 MiB of HBM per device.

```python
import math
import jax
import jax.numpy as jnp
from jax import lax

D = 1280
S = 256
TOKENS = 262144


def slot_table(key):
    base_key, gain_key = jax.random.split(key, 2)
    base = jnp.clip(jax.random.normal(base_key, (S // 2, 2, D), jnp.float32), -4.0, 4.0)
    gains = jnp.exp(jax.random.uniform(gain_key, (S // 2, 1), jnp.float32, math.log(0.3), math.log(3.0)))
    second = base[:, 1]
    first = base[:, 0]
    table = jnp.stack([first * gains, second * gains], axis=1) / math.sqrt(D)
    return table.reshape(S, D)


def draw_slot_embed(key, part):
    table = slot_table(key) * 0.07
    return table.astype(jnp.bfloat16)


def draw_tokens(key, part):
    key = jax.random.fold_in(key, 11)
    keys = jax.random.split(key, 2)
    place = jnp.arange(TOKENS, dtype=jnp.float32)[:, None]
    ramp = 0.6 + 1.2 * place / TOKENS
    row_scale = jnp.exp(jax.random.uniform(keys[0], (TOKENS, 1), jnp.float32, math.log(0.35), math.log(3.5)))
    drawn = jnp.clip(jax.random.normal(keys[1], (TOKENS, D), jnp.float32), -4.0, 4.0)
    rows = drawn * row_scale * ramp
    rows = jnp.clip(rows, -1000.0, 1000.0)
    return rows.astype(jnp.bfloat16)


def strengthened(result, key, source, target, parts, factor):
    owner, partner = [(jnp.arange(result.shape[axis_at]) // (result.shape[axis_at] // parts)).reshape([-1 if axis == axis_at else 1 for axis in range(result.ndim)]) for axis_at in (source, target)]
    chosen = jax.random.permutation(key, parts)[partner]
    strong = (owner == chosen) | (owner == (partner + parts // 2) % parts)
    return jnp.where(strong, factor * result, result)


def shard_levels(own_key, shape, cuts, least, high):
    def one(position, blocks):
        draws = jax.random.uniform(jax.random.fold_in(jax.random.fold_in(own_key, 6), position), (blocks,), jnp.float32, least / len(cuts), high / len(cuts))
        return jnp.repeat(jnp.exp(draws), shape[position] // blocks).reshape((-1,) + (1,) * (len(shape) - position - 1))

    level = one(*cuts[0])
    for cut in cuts[1:]:
        level = level * one(*cut)
    return level


def noise(own_key, dims, deviation, limit, cuts=(), held_as=jnp.bfloat16):
    result = deviation * jax.random.normal(own_key, dims, jnp.float32)
    if cuts:
        result = result * shard_levels(own_key, dims, cuts, -0.22, 0.18)
    return jnp.clip(result, -limit, limit).astype(held_as)


def noise_with(key, extent, deviation, bound, cuts, heavy, kind=jnp.bfloat16):
    entries = deviation * jax.random.normal(key, extent, jnp.float32)
    if cuts:
        entries = entries * shard_levels(key, extent, cuts, -0.22, 0.18)
    return jnp.clip(strengthened(entries, jax.random.fold_in(key, 3), *heavy), -bound, bound).astype(kind)


def setup_inputs(seed: int = 0) -> dict:
    key_list = jax.random.split(jax.random.key(seed), 6)
    tokens = draw_tokens(jax.random.fold_in(key_list[5], 71), 0)
    slot_embed = draw_slot_embed(jax.random.fold_in(key_list[5], 71), 0)
    slot_outputs = noise(key_list[2], (S, D), 1.0, 6.0, ((0, 16), (1, 32)))
    output_grad = noise_with(key_list[3], (TOKENS, D), 96.0, 2560.0, ((0, 512),), (0, 1, 256, 6.0))
    slot_input_grad = noise(key_list[4], (S, D), (12 * (TOKENS // S)), 73728.0, ((0, 16), (1, 32)))
    return dict(tokens=tokens, slot_embed=slot_embed, slot_outputs=slot_outputs, output_grad=output_grad, slot_input_grad=slot_input_grad)


def contract_last(left, right):
    return lax.dot_general(left, right, (((1,), (1,)), ((), ())), preferred_element_type=jnp.float32)


def contract_first(left, right):
    return lax.dot_general(left, right, (((0,), (0,)), ((), ())), preferred_element_type=jnp.float32)


def reference(tokens, slot_embed, slot_outputs, output_grad, slot_input_grad):
    logits = contract_last(tokens, slot_embed)
    col_max = jnp.max(logits, axis=0, keepdims=True)
    raised = jnp.exp(logits - col_max)
    dispatch = raised / jnp.sum(raised, axis=0, keepdims=True)
    combine = jax.nn.softmax(logits, axis=1)
    dispatch_grad = contract_last(tokens, slot_input_grad)
    combine_grad = contract_last(output_grad, slot_outputs)
    column_term = jnp.sum(dispatch * dispatch_grad, axis=0, keepdims=True)
    row_term = jnp.sum(combine * combine_grad, axis=1, keepdims=True)
    logit_grad = (combine * (combine_grad - row_term) + dispatch * (dispatch_grad - column_term)).astype(jnp.bfloat16)
    dispatch_low = dispatch.astype(jnp.bfloat16)
    combine_low = combine.astype(jnp.bfloat16)
    token_grad = (jnp.dot(logit_grad, slot_embed, preferred_element_type=jnp.float32)
                  + jnp.dot(dispatch_low, slot_input_grad, preferred_element_type=jnp.float32)).astype(jnp.bfloat16)
    embed_grad = contract_first(logit_grad, tokens)
    slot_output_grad = contract_first(combine_low, output_grad)
    return (token_grad, embed_grad, slot_output_grad)
```

```python
import jax
import jax.numpy as jnp
from jax import lax
from jax.sharding import Mesh, PartitionSpec as P

BF = jnp.bfloat16
F32 = jnp.float32
YZ = ("z", "core", "y")
X = ("xh", "xl")


def nt(a, b):
    return lax.dot_general(a, b, (((1,), (1,)), ((), ())), preferred_element_type=F32)


def nn(a, b):
    return lax.dot_general(a, b, (((1,), (0,)), ((), ())), preferred_element_type=F32)


def tn(a, b):
    return lax.dot_general(a, b, (((0,), (0,)), ((), ())), preferred_element_type=F32)


def low(x):
    return lax.reduce_precision(x, 8, 7)


def split3(x):
    a = low(x)
    b = low(x - a)
    return [a.astype(BF), b.astype(BF), (x - a - b).astype(BF)]


def pack(m, s, t):
    return jnp.stack(split3(m) + split3(s)[:2] + split3(t), axis=0)


def unpack(p):
    p = p.astype(F32)
    return p[0] + p[1] + p[2], p[3] + p[4], p[5] + p[6] + p[7]


def merge(m, s, t):
    top = jnp.max(m, axis=0)
    w = jnp.exp(m - top[None])
    ws = w * s
    total = jnp.sum(ws, axis=0)
    mean = jnp.sum(ws * t, axis=0) / total
    return top, total, mean, w, t - mean[None]


def merge_data(d, w, dt):
    d = d.astype(F32)
    w = w[:, :, None]
    dt = dt[:, :, None]
    o = jnp.sum(d[:, 0], 0)
    a = jnp.sum(d[:, 1], 0)
    b = jnp.sum(w * (d[:, 2] + dt * d[:, 3]), 0)
    c = jnp.sum(w * d[:, 3], 0)
    return jnp.stack([o, a, b, c], 0)


def swap(x):
    return lax.ppermute(x, "core", [(0, 1), (1, 0)])


def per_device(tokens, slot_embed, slot_outputs, output_grad, slot_input_grad):
    piece = jnp.stack([slot_embed, slot_outputs, slot_input_grad])
    piece = piece.reshape(3, 2, 8, 40).transpose(1, 0, 2, 3).reshape(1, 2, 1, 960)
    op = jnp.broadcast_to(piece, (8, 2, 8, 960)).reshape(128, 960)
    got = lax.all_to_all(op, YZ, 0, 0, tiled=True)
    got = got.reshape(8, 2, 8, 3, 8, 40).transpose(3, 4, 2, 0, 1, 5).reshape(192, 640)
    got = lax.all_to_all(jnp.broadcast_to(got[None], (4, 192, 640)), X, 0, 0, tiled=True)
    own = got
    sib = swap(got)
    full = jnp.stack([own, sib]).reshape(2, 2, 2, 3, 64, 640)
    full = full.transpose(3, 0, 2, 4, 1, 5).reshape(3, 256, 1280)
    embed_all, outputs_all, inputs_all = full[0], full[1], full[2]

    logits = nt(embed_all, tokens)
    dgrad = nt(inputs_all, tokens)
    cgrad = nt(outputs_all, output_grad)
    combine = jax.nn.softmax(logits, axis=0)
    row = jnp.sum(combine * cgrad, axis=0, keepdims=True)
    part = combine * (cgrad - row)
    m = jnp.max(logits, axis=1)
    e = jnp.exp(logits - m[:, None])
    s = jnp.sum(e, axis=1)
    t = jnp.sum(e * dgrad, axis=1) / s
    dc = dgrad - t[:, None]
    o = nn(combine.astype(BF), output_grad)
    a = nn(part.astype(BF), tokens)
    b = nn((e * dc).astype(BF), tokens)
    c = nn(e.astype(BF), tokens)
    data = jnp.stack([o, a, b, c]).astype(BF)

    st = pack(m, s, t)
    st2 = swap(st)
    st2 = jnp.concatenate([st2[:, 128:], st2[:, :128]], 1)
    d2 = swap(data[:, 128:])
    ms, ss, ts = unpack(jnp.stack([st, st2], 1))
    m1, s1, t1, w, dt = merge(ms, ss, ts)
    d = merge_data(jnp.stack([data[:, :128], d2]), w[:, :128], dt[:, :128]).astype(BF)

    d = d.reshape(4, 2, 64, 2, 640).transpose(3, 1, 0, 2, 4).reshape(4, 256, 640)
    st = jnp.pad(pack(m1, s1, t1), ((0, 8), (0, 384)))
    op = jnp.concatenate([d, jnp.broadcast_to(st[None], (4, 16, 640))], 1)
    got = lax.all_to_all(op, X, 0, 0, tiled=True)
    ms, ss, ts = unpack(got[:, 256:264, :256].transpose(1, 0, 2))
    m2, s2, t2, w, dt = merge(ms, ss, ts)
    xl = lax.axis_index("xl")
    wx = lax.dynamic_slice_in_dim(w[:, :128], xl * 64, 64, 1)
    dx = lax.dynamic_slice_in_dim(dt[:, :128], xl * 64, 64, 1)
    d = merge_data(got[:, :256].reshape(4, 4, 64, 640), wx, dx).astype(BF)

    d = d.reshape(4, 8, 8, 8, 2, 40).transpose(3, 4, 2, 0, 1, 5).reshape(128, 1280)
    st = pack(m2[:128], s2[:128], t2[:128]).reshape(1, 1024)
    op = jnp.concatenate([d, jnp.broadcast_to(st, (128, 1024))], 1)
    got = lax.all_to_all(op, YZ, 0, 0, tiled=True).reshape(8, 2, 8, 2304)
    got = got.transpose(0, 2, 1, 3).reshape(64, 2, 2304)
    ms, ss, ts = unpack(got[:, :, 1280:].reshape(64, 2, 8, 128).transpose(2, 0, 1, 3))
    M, S, T, w, dt = merge(ms, ss, ts)
    y = lax.axis_index("y")

    def mine(v):
        v = v.reshape(64, 2, 2, 8, 8)
        v = lax.dynamic_index_in_dim(v, xl, 2, keepdims=False)
        return lax.dynamic_index_in_dim(v, y, 3, keepdims=False).reshape(64, 16)

    d = got[:, :, :1280].reshape(64, 2, 4, 8, 40).transpose(0, 2, 1, 3, 4).reshape(64, 4, 16, 40)
    d = merge_data(d, mine(w), mine(dt))
    Sm = mine(jnp.broadcast_to(S[None], (64, 2, 128)))[0]
    embed_grad = d[1] + d[2] / Sm[:, None]
    out_grad = d[0]

    core = lax.axis_index("core")

    def rel(v):
        return jnp.concatenate([
            lax.dynamic_index_in_dim(v, core, 0, keepdims=False),
            lax.dynamic_index_in_dim(v, 1 - core, 0, keepdims=False)])

    M, S, T = rel(M), rel(S), rel(T)
    alpha = jnp.exp(m - M) / S
    disp = e * alpha[:, None]
    lg = (part + disp * (dc + (t - T)[:, None])).astype(BF)
    token_grad = (tn(lg, embed_all) + tn(disp.astype(BF), inputs_all)).astype(BF)
    return token_grad, embed_grad, out_grad


def solution(mesh):
    fine = Mesh(mesh.devices.reshape(2, 8, 2, 8, 2), ("xh", "z", "core", "y", "xl"))
    rows = P(("xh", "z", "core", "y", "xl"), None)
    slot = P(("y", "xl"), ("xh", "z", "core"))
    return jax.shard_map(
        per_device,
        mesh=fine,
        in_specs=(rows, slot, slot, rows, slot),
        out_specs=(rows, slot, slot),
        check_vma=False,
    )
```

```python
import jax
import jax.numpy as jnp
from jax import lax
from jax.experimental import pallas as pl
from jax.experimental.pallas import tpu as pltpu
from jax.sharding import Mesh, PartitionSpec as P

BF = jnp.bfloat16
F32 = jnp.float32
YZ = ("z", "core", "y")
X = ("xh", "xl")
LANES = 128
WIDE = 40
VMEM_BYTES = 32 * 1024 * 1024


def nt(a, b):
    return lax.dot_general(a, b, (((1,), (1,)), ((), ())), preferred_element_type=F32)


def nn(a, b):
    return lax.dot_general(a, b, (((1,), (0,)), ((), ())), preferred_element_type=F32)


def tn(a, b):
    return lax.dot_general(a, b, (((0,), (0,)), ((), ())), preferred_element_type=F32)


def roll(x, shift):
    shift %= LANES
    return x if shift == 0 else pltpu.roll(x, shift, axis=x.ndim - 1)


def lane_of(shape):
    return lax.broadcasted_iota(jnp.int32, shape, len(shape) - 1)


def columns(p, n, first):
    shape = (n, 8, LANES)
    pick = lane_of(shape) == lax.broadcasted_iota(jnp.int32, shape, 0) + first
    x = jnp.where(pick, jnp.broadcast_to(p[None], shape), 0.0)
    return jnp.sum(x, axis=2, keepdims=True).reshape(n * 8, 1)


def packed(v, n, first):
    shape = (n, 8, LANES)
    pick = lane_of(shape) == lax.broadcasted_iota(jnp.int32, shape, 0) + first
    x = jnp.where(pick, jnp.broadcast_to(v.reshape(n, 8, 1), shape), 0.0)
    return jnp.sum(x, axis=0)


def split(x, n):
    parts = []
    for _ in range(n):
        part = x.astype(BF)
        parts.append(part)
        x = x - part.astype(F32)
    return parts


def stat_rows(p):
    a, b, c = split(p, 3)
    rest = jnp.zeros((8, 640 - 3 * LANES), BF)
    top = jnp.concatenate([a, b, c, rest], axis=1).astype(F32)
    return jnp.concatenate([top, jnp.zeros((8, 640), F32)], axis=0).astype(BF)


def stat_read(rows):
    f = rows.astype(F32)[:8]
    return f[:, :LANES] + f[:, LANES:2 * LANES] + f[:, 2 * LANES:3 * LANES]


def pieces_kernel(e_ref, o_ref, i_ref, out_ref):
    def at(ref, k):
        x = ref[...].astype(F32)
        x = jnp.concatenate([x, jnp.zeros((16, LANES - WIDE), F32)], axis=1)
        return roll(x, k * WIDE)

    x = at(e_ref, 0) + at(o_ref, 1) + at(i_ref, 2)
    for half in range(2):
        rows = x[half * 8:half * 8 + 8]
        many = jnp.broadcast_to(rows[None], (8, 8, LANES)).astype(BF)
        for z in range(8):
            at_row = (z * 2 + half) * 8
            out_ref[at_row:at_row + 8] = many


def widen_kernel(got_ref, out_ref):
    lane = lane_of((64, LANES))
    blocks = [got_ref[k * 8:(k + 1) * 8].astype(F32).reshape(64, LANES) for k in range(16)]
    for a in range(3):
        tiles = [None] * 5
        for k in range(16):
            x = roll(blocks[k], WIDE * (k - a))
            first, last = WIDE * k, WIDE * k + WIDE
            for j in range(first // LANES, (last - 1) // LANES + 1):
                lo = max(first - j * LANES, 0)
                tiles[j] = x if tiles[j] is None else jnp.where(lane >= lo, x, tiles[j])
        whole = jnp.concatenate(tiles, axis=1).astype(BF)
        for j in range(4):
            out_ref[j, a * 64:(a + 1) * 64, :] = whole


def main_kernel(own_ref, sib_ref, tok_ref, og_ref,
                g_ref, e_ref, part_ref, dc_ref, m_ref, t_ref, p_ref, down_ref, dsib_ref, outs_ref):
    for h, ref in ((0, own_ref), (1, sib_ref)):
        for xl in range(2):
            for xh in range(2):
                rows = pl.ds(h * 128 + xl * 64, 64)
                cols = pl.ds(xh * 640, 640)
                j = xh * 2 + xl
                g_ref[rows, cols] = ref[j, 0:64, :]
                outs_ref[rows, cols] = ref[j, 64:128, :]
                g_ref[pl.ds(256 + h * 128 + xl * 64, 64), cols] = ref[j, 128:192, :]
    tok = tok_ref[...]
    og = og_ref[...]
    cgrad = nt(outs_ref[...], og)
    logits = nt(g_ref[0:256, :], tok)
    dgrad = nt(g_ref[256:512, :], tok)
    raised = jnp.exp(logits - jnp.max(logits, axis=0, keepdims=True))
    combine = raised / jnp.sum(raised, axis=0, keepdims=True)
    row = jnp.sum(combine * cgrad, axis=0, keepdims=True)
    part = combine * (cgrad - row)
    m = jnp.max(logits, axis=1, keepdims=True)
    e = jnp.exp(logits - m)
    s = jnp.sum(e, axis=1, keepdims=True)
    t = jnp.sum(e * dgrad, axis=1, keepdims=True) / s
    dc = dgrad - t
    e_ref[...] = e
    part_ref[...] = part
    dc_ref[...] = dc
    m_ref[...] = m
    t_ref[...] = t
    p = packed(m, 32, 0) + packed(s, 32, 32) + packed(t, 32, 64)
    p_ref[...] = p
    for k, (left, right) in enumerate(((combine, og), (part, tok), (e * dc, tok), (e, tok))):
        x = nn(left.astype(BF), right).astype(BF)
        down_ref[k * 128:(k + 1) * 128, :] = x[:128]
        dsib_ref[k * 128:(k + 1) * 128, :] = x[128:]
    dsib_ref[512:528, 0:640] = stat_rows(p)
    dsib_ref[512:528, 640:1280] = jnp.zeros((16, 640), BF)


def merge_stats(ps, groups, exact=True):
    ms = ps
    ss = [roll(p, -groups) for p in ps]
    ts = [roll(p, -2 * groups) for p in ps]
    lane = lane_of((8, LANES))
    ok = lane < groups
    ms = [jnp.where(ok, v, 0.0) for v in ms]
    ss = [jnp.where(ok, v, 1.0) for v in ss]
    ts = [jnp.where(ok, v, 0.0) for v in ts]
    top = ms[0]
    for v in ms[1:]:
        top = jnp.maximum(top, v)
    if not exact:
        top = sum(v.astype(F32) for v in split(top, 2))
    ws = [jnp.exp(v - top) for v in ms]
    total = sum(w * s for w, s in zip(ws, ss))
    mean = sum(w * s * t for w, s, t in zip(ws, ss, ts)) / total
    if not exact:
        mean = sum(v.astype(F32) for v in split(mean, 2))
    return top, total, mean, ws, [t - mean for t in ts]


def core_kernel(own_ref, got_ref, p_ref, out_ref):
    lane = lane_of((8, LANES))
    q = stat_read(got_ref[512:528, 0:640])
    q = jnp.where(lane % 32 < 16, roll(q, -16), roll(q, 16))
    top, total, mean, ws, ds = merge_stats([p_ref[...], q], 32)
    ok = lane < 32
    p = jnp.where(ok, top, 0.0) + roll(jnp.where(ok, total, 0.0), 32) + roll(jnp.where(ok, mean, 0.0), 64)
    stats = stat_rows(p)
    w1, w2 = columns(ws[0], 16, 0), columns(ws[1], 16, 0)
    d1, d2 = columns(ds[0], 16, 0), columns(ds[1], 16, 0)

    def rows(ref, k):
        return ref[k * 128:(k + 1) * 128, :].astype(F32)

    def put(k, x):
        x = x.astype(BF)
        for xh in range(2):
            for xl in range(2):
                out_ref[xh * 2 + xl, k * 64:(k + 1) * 64, :] = x[xl * 64:(xl + 1) * 64, xh * 640:(xh + 1) * 640]

    put(0, rows(own_ref, 0) + rows(got_ref, 0))
    put(1, rows(own_ref, 1) + rows(got_ref, 1))
    c1, c2 = w1 * rows(own_ref, 3), w2 * rows(got_ref, 3)
    put(2, w1 * rows(own_ref, 2) + w2 * rows(got_ref, 2) + d1 * c1 + d2 * c2)
    put(3, c1 + c2)
    for j in range(4):
        out_ref[j, 256:272, :] = stats


def x_kernel(got_ref, out_ref):
    xl = lax.axis_index("xl")
    top, total, mean, ws, ds = merge_stats([stat_read(got_ref[j, 256:272, :]) for j in range(4)], 32, False)
    ws = [columns(w, 8, xl * 8) for w in ws]
    ds = [columns(d, 8, xl * 8) for d in ds]

    def rows(j, k):
        return got_ref[j, k * 64:(k + 1) * 64, :].astype(F32)

    o = sum(rows(j, 0) for j in range(4))
    a = sum(rows(j, 1) for j in range(4))
    cs = [ws[j] * rows(j, 3) for j in range(4)]
    b = sum(ws[j] * rows(j, 2) + ds[j] * cs[j] for j in range(4))
    c = sum(cs)
    lane8 = lane_of((8, LANES))
    ok = lane8 < 16
    p = jnp.where(ok, top, 0.0) + roll(jnp.where(ok, total, 0.0), 16) + roll(jnp.where(ok, mean, 0.0), 32)
    hi, mid = split(p, 2)
    stats = roll(hi.astype(F32), 32) + roll(mid.astype(F32), 80)
    stats = jnp.broadcast_to(stats[None], (8, 8, LANES)).reshape(64, LANES)
    lane = lane_of((64, LANES))
    for k in range(16):
        first = WIDE * k
        j = first // LANES
        cut = (j + 1) * LANES - first
        chunks = []
        for n, x in enumerate((o, a, b, c)):
            v = x[:, j * LANES:(j + 1) * LANES]
            if cut < WIDE:
                v = jnp.where(lane < WIDE - cut, x[:, (j + 1) * LANES:(j + 2) * LANES], v)
            chunks.append(roll(v, WIDE * n - first))
        low = jnp.where(lane < 40, chunks[0], jnp.where(lane < 80, chunks[1], jnp.where(lane < 120, chunks[2], chunks[3])))
        high = jnp.where(lane < 32, chunks[3], stats)
        out_ref[k * 8:(k + 1) * 8, :, 0:LANES] = low.reshape(8, 8, LANES).astype(BF)
        out_ref[k * 8:(k + 1) * 8, :, LANES:2 * LANES] = high.reshape(8, 8, LANES).astype(BF)


def last_kernel(got_ref, g_ref, e_ref, part_ref, dc_ref, m_ref, t_ref, tg_ref, eg_ref, og_ref, l_ref):
    xl, y, core = lax.axis_index("xl"), lax.axis_index("y"), lax.axis_index("core")
    big = (8, 2, 8, 8, LANES)
    t0 = got_ref[:, :, 0:LANES].astype(F32).reshape(big)
    t1 = got_ref[:, :, LANES:2 * LANES].astype(F32).reshape(1024, LANES)
    p = t1 + roll(t1, -48)
    s = roll(p, -16).reshape(big)
    t = roll(p, -32).reshape(big)
    m = p.reshape(big)
    t1 = t1.reshape(big)
    lane = lane_of((8, LANES))
    ok = (lane >= 32) & (lane < 48)
    m = jnp.where(ok, m, 0.0)
    s = jnp.where(ok, s, 1.0)
    t = jnp.where(ok, t, 0.0)
    top = jnp.max(m, axis=(0, 2))
    w = jnp.exp(m - top[None, :, None])
    ws = w * s
    total = jnp.sum(ws, axis=(0, 2))
    mean = jnp.sum(ws * t, axis=(0, 2)) / total
    dt = t - mean[None, :, None]
    mine = lane == 32 + xl * 8 + y

    def pick(v):
        return jnp.sum(jnp.where(mine, v, 0.0), axis=-1, keepdims=True)

    wm = pick(w)
    wd = wm * pick(dt)
    acc0 = jnp.sum(t0 * jnp.where(lane < 80, 1.0, jnp.where(lane < 120, wm, wd)), axis=(0, 2))
    acc1 = jnp.sum(jnp.where(lane < 32, t1 * wd, 0.0), axis=(0, 2))
    for c in range(2):
        q = acc0[c]
        last = jnp.where(lane < 8, roll(q, -120), roll(acc1[c], 8))
        grad = roll(q, -40) + (roll(q, -80) + last) / pick(total[c])
        eg_ref[c * 8:(c + 1) * 8, :] = grad[:, 0:WIDE]
        og_ref[c * 8:(c + 1) * 8, :] = q[:, 0:WIDE]

    for h in range(2):
        second = (core + h) == 1

        def cols(v):
            return columns(jnp.where(second, v[1], v[0]), 16, 32)

        at = pl.ds(h * 128, 128)
        alpha = jnp.exp(m_ref[at, :] - cols(top)) / cols(total)
        shift = t_ref[at, :] - cols(mean)
        disp = e_ref[at, :] * alpha
        l_ref[at, :] = (part_ref[at, :] + disp * (dc_ref[at, :] + shift)).astype(BF)
        l_ref[pl.ds(256 + h * 128, 128), :] = disp.astype(BF)
    tg_ref[...] = tn(l_ref[...], g_ref[...]).astype(BF)


def call(kernel, outs, *args, scratch=(), flops=0):
    vm = pl.BlockSpec(memory_space=pltpu.VMEM)
    many = isinstance(outs, list)
    return pl.pallas_call(
        kernel,
        out_shape=outs,
        in_specs=[vm] * len(args),
        out_specs=[vm] * len(outs) if many else vm,
        scratch_shapes=list(scratch),
        compiler_params=pltpu.CompilerParams(vmem_limit_bytes=VMEM_BYTES),
    )(*args)


def shape(*dims, dtype=BF):
    return jax.ShapeDtypeStruct(dims, dtype)


def swap(x):
    return lax.ppermute(x, "core", [(0, 1), (1, 0)])


def per_device(tokens, slot_embed, slot_outputs, output_grad, slot_input_grad):
    op = call(pieces_kernel, shape(128, 8, LANES), slot_embed, slot_outputs, slot_input_grad)
    got = lax.all_to_all(op, YZ, 0, 0, tiled=True)
    op = call(widen_kernel, shape(4, 192, 640), got)
    own = lax.all_to_all(op, X, 0, 0, tiled=True)
    sib = swap(own)
    g, e, part, dc, m, t, p, down, dsib = call(
        main_kernel,
        [shape(512, 1280), shape(256, 512, dtype=F32), shape(256, 512, dtype=F32), shape(256, 512, dtype=F32),
         shape(256, 1, dtype=F32), shape(256, 1, dtype=F32), shape(8, LANES, dtype=F32),
         shape(512, 1280), shape(528, 1280)],
        own, sib, tokens, output_grad,
        scratch=[pltpu.VMEM((256, 1280), BF)])
    op = call(core_kernel, shape(4, 272, 640), down, swap(dsib), p)
    got = lax.all_to_all(op, X, 0, 0, tiled=True)
    op = call(x_kernel, shape(128, 8, 2 * LANES), got)
    got = lax.all_to_all(op, YZ, 0, 0, tiled=True)
    return call(
        last_kernel,
        [shape(512, 1280), shape(16, WIDE, dtype=F32), shape(16, WIDE, dtype=F32)],
        got, g, e, part, dc, m, t,
        scratch=[pltpu.VMEM((512, 512), BF)])


def solution(mesh):
    fine = Mesh(mesh.devices.reshape(2, 8, 2, 8, 2), ("xh", "z", "core", "y", "xl"))
    rows = P(("xh", "z", "core", "y", "xl"), None)
    slot = P(("y", "xl"), ("xh", "z", "core"))
    return jax.shard_map(
        per_device,
        mesh=fine,
        in_specs=(rows, slot, slot, rows, slot),
        out_specs=(rows, slot, slot),
        check_vma=False,
    )
```

```python
import jax
import jax.numpy as jnp
from jax import lax
from jax.experimental import pallas as pl
from jax.experimental.pallas import tpu as pltpu
from jax.sharding import Mesh, PartitionSpec as P

BF = jnp.bfloat16
F32 = jnp.float32
YZ = ("z", "core", "y")
X = ("xh", "xl")
LANES = 128
WIDE = 40
VMEM_BYTES = 16 * 1024 * 1024


def nt(a, b):
    return lax.dot_general(a, b, (((1,), (1,)), ((), ())), preferred_element_type=F32)


def nn(a, b):
    return lax.dot_general(a, b, (((1,), (0,)), ((), ())), preferred_element_type=F32)


def tn(a, b):
    return lax.dot_general(a, b, (((0,), (0,)), ((), ())), preferred_element_type=F32)


def roll(x, shift):
    shift %= LANES
    return x if shift == 0 else pltpu.roll(x, shift, axis=x.ndim - 1)


def lane_of(shape):
    return lax.broadcasted_iota(jnp.int32, shape, len(shape) - 1)


def columns(p, n, first):
    shape = (n, 8, LANES)
    pick = lane_of(shape) == lax.broadcasted_iota(jnp.int32, shape, 0) + first
    x = jnp.where(pick, jnp.broadcast_to(p[None], shape), 0.0)
    return jnp.sum(x, axis=2, keepdims=True).reshape(n * 8, 1)


def packed(v, n, first):
    shape = (n, 8, LANES)
    pick = lane_of(shape) == lax.broadcasted_iota(jnp.int32, shape, 0) + first
    x = jnp.where(pick, jnp.broadcast_to(v.reshape(n, 8, 1), shape), 0.0)
    return jnp.sum(x, axis=0)


def split(x, n):
    parts = []
    for _ in range(n):
        part = x.astype(BF)
        parts.append(part)
        x = x - part.astype(F32)
    return parts


def stat_rows(p):
    a, b, c = split(p, 3)
    rest = jnp.zeros((8, 640 - 3 * LANES), BF)
    top = jnp.concatenate([a, b, c, rest], axis=1).astype(F32)
    return jnp.concatenate([top, jnp.zeros((8, 640), F32)], axis=0).astype(BF)


def stat_read(rows):
    f = rows.astype(F32)[:8]
    return f[:, :LANES] + f[:, LANES:2 * LANES] + f[:, 2 * LANES:3 * LANES]


def pieces_kernel(e_ref, o_ref, i_ref, out_ref, in_ref, sems):
    copies = [pltpu.make_async_copy(ref, in_ref.at[k], sems.at[k]) for k, ref in enumerate((e_ref, o_ref, i_ref))]
    for copy in copies:
        copy.start()
    for copy in copies:
        copy.wait()

    def at(k):
        x = in_ref[k].astype(F32)
        x = jnp.concatenate([x, jnp.zeros((16, LANES - WIDE), F32)], axis=1)
        return roll(x, k * WIDE)

    x = at(0) + at(1) + at(2)
    for half in range(2):
        rows = x[half * 8:half * 8 + 8]
        many = jnp.broadcast_to(rows[None], (8, 8, LANES)).astype(BF)
        for z in range(8):
            at_row = (z * 2 + half) * 8
            out_ref[at_row:at_row + 8] = many


def widen_kernel(got_ref, out_ref):
    lane = lane_of((64, LANES))
    blocks = [got_ref[k * 8:(k + 1) * 8].astype(F32).reshape(64, LANES) for k in range(16)]
    for a in range(3):
        tiles = [None] * 5
        for k in range(16):
            x = roll(blocks[k], WIDE * (k - a))
            first, last = WIDE * k, WIDE * k + WIDE
            for j in range(first // LANES, (last - 1) // LANES + 1):
                lo = max(first - j * LANES, 0)
                tiles[j] = x if tiles[j] is None else jnp.where(lane >= lo, x, tiles[j])
        whole = jnp.concatenate(tiles, axis=1).astype(BF)
        for j in range(4):
            out_ref[j, a * 64:(a + 1) * 64, :] = whole


def scores_kernel(got_ref, tok_ref, tok2_ref, og_ref, og2_ref, g_ref, lg_ref, dg_ref, cg_ref, r_ref, outs_ref):
    for xl in range(2):
        for xh in range(2):
            at, cols, j = xl * 64, pl.ds(xh * 640, 640), xh * 2 + xl
            g_ref[at:at + 64, cols] = got_ref[j, 0:64, :]
            outs_ref[at:at + 64, cols] = got_ref[j, 64:128, :]
            g_ref[128 + at:192 + at, cols] = got_ref[j, 128:192, :]
    g = g_ref[...]
    outs = outs_ref[...]
    r_ref[...] = jnp.zeros_like(r_ref)
    for h, (tok, og) in enumerate(((tok_ref, og_ref), (tok2_ref, og2_ref))):
        cols = pl.ds(h * 512, 512)
        both = nt(g, tok[...])
        cgrad = nt(outs, og[...])
        logits = both[:128]
        lg_ref[:, cols] = logits
        dg_ref[:, cols] = both[128:]
        cg_ref[:, cols] = cgrad
        top = jnp.max(logits, axis=0, keepdims=True)
        raised = jnp.exp(logits - top)
        r_ref[0:1, cols] = top
        r_ref[1:2, cols] = jnp.sum(raised, axis=0, keepdims=True)
        r_ref[2:3, cols] = jnp.sum(raised * cgrad, axis=0, keepdims=True)


def slots_kernel(lg_ref, dg_ref, tok_ref, tok2_ref, e_ref, dc_ref, p_ref, bc_ref):
    logits = lg_ref[...]
    dgrad = dg_ref[...]
    m = jnp.max(logits, axis=1, keepdims=True)
    e = jnp.exp(logits - m)
    s = jnp.sum(e, axis=1, keepdims=True)
    t = jnp.sum(e * dgrad, axis=1, keepdims=True) / s
    dc = dgrad - t
    e_ref[...] = e
    dc_ref[...] = dc
    p_ref[...] = packed(m, 16, 0) + packed(s, 16, 16) + packed(t, 16, 32)
    left = jnp.concatenate([(e * dc).astype(BF), e.astype(BF)], axis=0)
    bc_ref[...] = (nn(left[:, :512], tok_ref[...]) + nn(left[:, 512:], tok2_ref[...])).astype(BF)


def tokens_kernel(lg_ref, cg_ref, r_ref, r2_ref, e_ref, dc_ref, p_ref, bc_ref, tok_ref, tok2_ref, og_ref, og2_ref,
                  out_ref, keep_ref, send_ref):
    def put(k, x):
        for xh in range(2):
            for xl in range(2):
                out_ref[xh * 2 + xl, k * 64:(k + 1) * 64, :] = x[xl * 64:(xl + 1) * 64, xh * 640:(xh + 1) * 640]

    o = a = None
    for h, (tok, og, keep) in enumerate(((tok_ref, og_ref, keep_ref), (tok2_ref, og2_ref, send_ref))):
        cols = pl.ds(h * 512, 512)
        other = pl.ds((1 - h) * 512, 512)
        m1, m2 = r_ref[0:1, cols], r2_ref[0:1, other]
        top = jnp.maximum(m1, m2)
        w1, w2 = jnp.exp(m1 - top), jnp.exp(m2 - top)
        total = w1 * r_ref[1:2, cols] + w2 * r2_ref[1:2, other]
        row = (w1 * r_ref[2:3, cols] + w2 * r2_ref[2:3, other]) / total
        combine = jnp.exp(lg_ref[:, cols] - top) / total
        part = combine * (cg_ref[:, cols] - row)
        keep[0:128, :] = e_ref[:, cols]
        keep[128:256, :] = part
        keep[256:384, :] = dc_ref[:, cols]
        keep[384:392, 0:LANES] = p_ref[...]
        keep[384:392, LANES:512] = jnp.zeros((8, 512 - LANES), F32)
        o1 = nn(combine.astype(BF), og[...])
        a1 = nn(part.astype(BF), tok[...])
        o, a = (o1, a1) if h == 0 else (o + o1, a + a1)
    put(0, o.astype(BF))
    put(1, a.astype(BF))
    put(2, bc_ref[0:128, :])
    put(3, bc_ref[128:256, :])
    stats = stat_rows(p_ref[...])
    for j in range(4):
        out_ref[j, 256:272, :] = stats


def merge_stats(ps, groups, exact=True):
    ms = ps
    ss = [roll(p, -groups) for p in ps]
    ts = [roll(p, -2 * groups) for p in ps]
    lane = lane_of((8, LANES))
    ok = lane < groups
    ms = [jnp.where(ok, v, 0.0) for v in ms]
    ss = [jnp.where(ok, v, 1.0) for v in ss]
    ts = [jnp.where(ok, v, 0.0) for v in ts]
    top = ms[0]
    for v in ms[1:]:
        top = jnp.maximum(top, v)
    if not exact:
        top = sum(v.astype(F32) for v in split(top, 2))
    ws = [jnp.exp(v - top) for v in ms]
    total = sum(w * s for w, s in zip(ws, ss))
    mean = sum(w * s * t for w, s, t in zip(ws, ss, ts)) / total
    if not exact:
        mean = sum(v.astype(F32) for v in split(mean, 2))
    return top, total, mean, ws, [t - mean for t in ts]


def x_kernel(got_ref, out_ref):
    xl = lax.axis_index("xl")
    top, total, mean, ws, ds = merge_stats([stat_read(got_ref[j, 256:272, :]) for j in range(4)], 16, False)
    ws = [columns(w, 8, xl * 8) for w in ws]
    ds = [columns(d, 8, xl * 8) for d in ds]

    def rows(j, k):
        return got_ref[j, k * 64:(k + 1) * 64, :].astype(F32)

    o = sum(rows(j, 0) for j in range(4))
    a = sum(rows(j, 1) for j in range(4))
    cs = [ws[j] * rows(j, 3) for j in range(4)]
    b = sum(ws[j] * rows(j, 2) + ds[j] * cs[j] for j in range(4))
    c = sum(cs)
    lane8 = lane_of((8, LANES))
    ok = lane8 < 16
    p = jnp.where(ok, top, 0.0) + roll(jnp.where(ok, total, 0.0), 16) + roll(jnp.where(ok, mean, 0.0), 32)
    hi, mid = split(p, 2)
    stats = roll(hi.astype(F32), 32) + roll(mid.astype(F32), 80)
    stats = jnp.broadcast_to(stats[None], (8, 8, LANES)).reshape(64, LANES)
    lane = lane_of((64, LANES))
    for k in range(16):
        first = WIDE * k
        j = first // LANES
        cut = (j + 1) * LANES - first
        chunks = []
        for n, x in enumerate((o, a, b, c)):
            v = x[:, j * LANES:(j + 1) * LANES]
            if cut < WIDE:
                v = jnp.where(lane < WIDE - cut, x[:, (j + 1) * LANES:(j + 2) * LANES], v)
            chunks.append(roll(v, WIDE * n - first))
        low = jnp.where(lane < 40, chunks[0], jnp.where(lane < 80, chunks[1], jnp.where(lane < 120, chunks[2], chunks[3])))
        high = jnp.where(lane < 32, chunks[3], stats)
        out_ref[k * 8:(k + 1) * 8, :, 0:LANES] = low.reshape(8, 8, LANES).astype(BF)
        out_ref[k * 8:(k + 1) * 8, :, LANES:2 * LANES] = high.reshape(8, 8, LANES).astype(BF)


def last_kernel(got_ref, g_ref, g2_ref, keep_ref, keep2_ref, tg_ref, eg_ref, og_ref):
    xl, y, core = lax.axis_index("xl"), lax.axis_index("y"), lax.axis_index("core")
    big = (8, 2, 8, 8, LANES)
    t0 = got_ref[:, :, 0:LANES].astype(F32).reshape(big)
    t1 = got_ref[:, :, LANES:2 * LANES].astype(F32).reshape(1024, LANES)
    p = t1 + roll(t1, -48)
    s = roll(p, -16).reshape(big)
    t = roll(p, -32).reshape(big)
    m = p.reshape(big)
    t1 = t1.reshape(big)
    lane = lane_of((8, LANES))
    ok = (lane >= 32) & (lane < 48)
    m = jnp.where(ok, m, 0.0)
    s = jnp.where(ok, s, 1.0)
    t = jnp.where(ok, t, 0.0)
    top = jnp.max(m, axis=(0, 2))
    w = jnp.exp(m - top[None, :, None])
    ws = w * s
    total = jnp.sum(ws, axis=(0, 2))
    mean = jnp.sum(ws * t, axis=(0, 2)) / total
    dt = t - mean[None, :, None]
    mine = lane == 32 + xl * 8 + y

    def pick(v):
        return jnp.sum(jnp.where(mine, v, 0.0), axis=-1, keepdims=True)

    wm = pick(w)
    wd = wm * pick(dt)
    acc0 = jnp.sum(t0 * jnp.where(lane < 80, 1.0, jnp.where(lane < 120, wm, wd)), axis=(0, 2))
    acc1 = jnp.sum(jnp.where(lane < 32, t1 * wd, 0.0), axis=(0, 2))
    for c in range(2):
        q = acc0[c]
        last = jnp.where(lane < 8, roll(q, -120), roll(acc1[c], 8))
        grad = roll(q, -40) + (roll(q, -80) + last) / pick(total[c])
        eg_ref[c * 8:(c + 1) * 8, :] = grad[:, 0:WIDE]
        og_ref[c * 8:(c + 1) * 8, :] = q[:, 0:WIDE]

    total_grad = None
    for h, (gr, kr) in enumerate(((g_ref, keep_ref), (g2_ref, keep2_ref))):
        second = (core + h) == 1

        def cols(v):
            return columns(jnp.where(second, v[1], v[0]), 16, 32)

        q = kr[384:392, 0:LANES]
        alpha = jnp.exp(columns(q, 16, 0) - cols(top)) / cols(total)
        shift = columns(q, 16, 32) - cols(mean)
        disp = kr[0:128, :] * alpha
        grad = kr[128:256, :] + disp * (kr[256:384, :] + shift)
        left = jnp.concatenate([grad.astype(BF), disp.astype(BF)], axis=0)
        x = tn(left, gr[...])
        total_grad = x if h == 0 else total_grad + x
    tg_ref[...] = total_grad.astype(BF)


def call(kernel, outs, *args, scratch=(), flops=0):
    vm = pl.BlockSpec(memory_space=pltpu.VMEM)
    many = isinstance(outs, list)
    return pl.pallas_call(
        kernel,
        out_shape=outs,
        in_specs=[vm] * len(args),
        out_specs=[vm] * len(outs) if many else vm,
        scratch_shapes=list(scratch),
        compiler_params=pltpu.CompilerParams(vmem_limit_bytes=VMEM_BYTES),
    )(*args)


def shape(*dims, dtype=BF):
    return jax.ShapeDtypeStruct(dims, dtype)


def swap(x):
    return lax.ppermute(x, "core", [(0, 1), (1, 0)])


def per_device(tokens, slot_embed, slot_outputs, output_grad, slot_input_grad):
    f32 = jnp.float32
    op = pl.pallas_call(
        pieces_kernel,
        out_shape=shape(128, 8, LANES),
        in_specs=[pl.BlockSpec(memory_space=pl.ANY)] * 3,
        out_specs=pl.BlockSpec(memory_space=pltpu.VMEM),
        scratch_shapes=[pltpu.VMEM((3, 16, WIDE), BF), pltpu.SemaphoreType.DMA((3,))],
        compiler_params=pltpu.CompilerParams(vmem_limit_bytes=60 * 1024 * 1024),
    )(slot_embed, slot_outputs, slot_input_grad)
    op, tok1 = lax.optimization_barrier((op, tokens))
    tok2 = swap(tok1)
    got = lax.all_to_all(op, YZ, 0, 0, tiled=True)
    op = call(widen_kernel, shape(4, 192, 640), got)
    op, og1 = lax.optimization_barrier((op, output_grad))
    og2 = swap(og1)
    got = lax.all_to_all(op, X, 0, 0, tiled=True)
    wide = shape(128, 1024, dtype=f32)
    g, lg, dg, cg, r = call(
        scores_kernel, [shape(256, 1280), wide, wide, wide, shape(8, 1024, dtype=f32)],
        got, tokens, tok2, output_grad, og2, scratch=[pltpu.VMEM((128, 1280), BF)])
    r2 = swap(r)
    e, dc, p, bc = call(
        slots_kernel, [wide, wide, shape(8, LANES, dtype=f32), shape(256, 1280)], lg, dg, tokens, tok2)
    op, keep, send = call(
        tokens_kernel, [shape(4, 272, 640), shape(392, 512, dtype=f32), shape(392, 512, dtype=f32)],
        lg, cg, r, r2, e, dc, p, bc, tokens, tok2, output_grad, og2)
    got = lax.all_to_all(op, X, 0, 0, tiled=True)
    g2, keep2 = swap(g), swap(send)
    op = call(x_kernel, shape(128, 8, 2 * LANES), got)
    got = lax.all_to_all(op, YZ, 0, 0, tiled=True)
    return call(
        last_kernel,
        [shape(512, 1280), shape(16, WIDE, dtype=f32), shape(16, WIDE, dtype=f32)],
        got, g, g2, keep, keep2)


def solution(mesh):
    fine = Mesh(mesh.devices.reshape(2, 8, 2, 8, 2), ("xh", "z", "core", "y", "xl"))
    rows = P(("xh", "z", "core", "y", "xl"), None)
    slot = P(("y", "xl"), ("xh", "z", "core"))
    return jax.shard_map(
        per_device,
        mesh=fine,
        in_specs=(rows, slot, slot, rows, slot),
        out_specs=(rows, slot, slot),
        check_vma=False,
    )
```

```python
import jax
import jax.numpy as jnp
from jax import lax
from jax.experimental import pallas as pl
from jax.experimental.pallas import tpu as pltpu
from jax.sharding import Mesh, PartitionSpec as P

BF = jnp.bfloat16
F32 = jnp.float32
YZ = ("z", "core", "y")
X = ("xh", "xl")
LANES = 128
WIDE = 40
VMEM_BYTES = 16 * 1024 * 1024


def nt(a, b):
    return lax.dot_general(a, b, (((1,), (1,)), ((), ())), preferred_element_type=F32)


def nn(a, b):
    return lax.dot_general(a, b, (((1,), (0,)), ((), ())), preferred_element_type=F32)


def tn(a, b):
    return lax.dot_general(a, b, (((0,), (0,)), ((), ())), preferred_element_type=F32)


def roll(x, shift):
    shift %= LANES
    return x if shift == 0 else pltpu.roll(x, shift, axis=x.ndim - 1)


def lane_of(shape):
    return lax.broadcasted_iota(jnp.int32, shape, len(shape) - 1)


def columns(p, n, first):
    shape = (n, 8, LANES)
    pick = lane_of(shape) == lax.broadcasted_iota(jnp.int32, shape, 0) + first
    x = jnp.where(pick, jnp.broadcast_to(p[None], shape), 0.0)
    return jnp.sum(x, axis=2, keepdims=True).reshape(n * 8, 1)


def packed(v, n, first):
    shape = (n, 8, LANES)
    pick = lane_of(shape) == lax.broadcasted_iota(jnp.int32, shape, 0) + first
    x = jnp.where(pick, jnp.broadcast_to(v.reshape(n, 8, 1), shape), 0.0)
    return jnp.sum(x, axis=0)


def split(x, n):
    parts = []
    for _ in range(n):
        part = x.astype(BF)
        parts.append(part)
        x = x - part.astype(F32)
    return parts


def stat_rows(p):
    a, b, c = split(p, 3)
    rest = jnp.zeros((8, 640 - 3 * LANES), BF)
    top = jnp.concatenate([a, b, c, rest], axis=1).astype(F32)
    return jnp.concatenate([top, jnp.zeros((8, 640), F32)], axis=0).astype(BF)


def stat_read(rows):
    f = rows.astype(F32)[:8]
    return f[:, :LANES] + f[:, LANES:2 * LANES] + f[:, 2 * LANES:3 * LANES]


def pieces_kernel(e_ref, o_ref, i_ref, out_ref, in_ref, sems):
    copies = [pltpu.make_async_copy(ref, in_ref.at[k], sems.at[k]) for k, ref in enumerate((e_ref, o_ref, i_ref))]
    for copy in copies:
        copy.start()
    for copy in copies:
        copy.wait()

    def at(k):
        x = in_ref[k].astype(F32)
        x = jnp.concatenate([x, jnp.zeros((16, LANES - WIDE), F32)], axis=1)
        return roll(x, k * WIDE)

    x = at(0) + at(1) + at(2)
    for half in range(2):
        rows = x[half * 8:half * 8 + 8]
        many = jnp.broadcast_to(rows[None], (8, 8, LANES)).astype(BF)
        for z in range(8):
            at_row = (z * 2 + half) * 8
            out_ref[at_row:at_row + 8] = many


def widen_kernel(got_ref, out_ref):
    lane = lane_of((64, LANES))
    blocks = [got_ref[k * 8:(k + 1) * 8].astype(F32).reshape(64, LANES) for k in range(16)]
    for a in range(3):
        tiles = [None] * 5
        for k in range(16):
            x = roll(blocks[k], WIDE * (k - a))
            first, last = WIDE * k, WIDE * k + WIDE
            for j in range(first // LANES, (last - 1) // LANES + 1):
                lo = max(first - j * LANES, 0)
                tiles[j] = x if tiles[j] is None else jnp.where(lane >= lo, x, tiles[j])
        whole = jnp.concatenate(tiles, axis=1).astype(BF)
        for j in range(4):
            out_ref[j, a * 64:(a + 1) * 64, :] = whole


def scores_kernel(got_ref, tok_ref, tok2_ref, og_ref, og2_ref, g_ref, lg_ref, dg_ref, cg_ref, r_ref, outs_ref):
    for xl in range(2):
        for xh in range(2):
            at, cols, j = xl * 64, pl.ds(xh * 640, 640), xh * 2 + xl
            g_ref[at:at + 64, cols] = got_ref[j, 0:64, :]
            outs_ref[at:at + 64, cols] = got_ref[j, 64:128, :]
            g_ref[128 + at:192 + at, cols] = got_ref[j, 128:192, :]
    g = g_ref[...]
    outs = outs_ref[...]
    r_ref[...] = jnp.zeros_like(r_ref)
    for h, (tok, og) in enumerate(((tok_ref, og_ref), (tok2_ref, og2_ref))):
        cols = pl.ds(h * 512, 512)
        both = nt(g, tok[...])
        cgrad = nt(outs, og[...])
        logits = both[:128]
        lg_ref[:, cols] = logits
        dg_ref[:, cols] = both[128:]
        cg_ref[:, cols] = cgrad
        top = jnp.max(logits, axis=0, keepdims=True)
        raised = jnp.exp(logits - top)
        r_ref[0:1, cols] = top
        r_ref[1:2, cols] = jnp.sum(raised, axis=0, keepdims=True)
        r_ref[2:3, cols] = jnp.sum(raised * cgrad, axis=0, keepdims=True)


def slots_kernel(lg_ref, dg_ref, tok_ref, tok2_ref, e_ref, dc_ref, p_ref, bc_ref):
    logits = lg_ref[...]
    dgrad = dg_ref[...]
    m = jnp.max(logits, axis=1, keepdims=True)
    e = jnp.exp(logits - m)
    s = jnp.sum(e, axis=1, keepdims=True)
    t = jnp.sum(e * dgrad, axis=1, keepdims=True) / s
    dc = dgrad - t
    e_ref[...] = e
    dc_ref[...] = dc
    p_ref[...] = packed(m, 16, 0) + packed(s, 16, 16) + packed(t, 16, 32)
    left = jnp.concatenate([(e * dc).astype(BF), e.astype(BF)], axis=0)
    bc_ref[...] = (nn(left[:, :512], tok_ref[...]) + nn(left[:, 512:], tok2_ref[...])).astype(BF)


def tokens_kernel(lg_ref, cg_ref, r_ref, r2_ref, e_ref, dc_ref, p_ref, bc_ref, tok_ref, tok2_ref, og_ref, og2_ref,
                  out_ref, keep_ref, send_ref):
    def put(k, x):
        for xh in range(2):
            for xl in range(2):
                out_ref[xh * 2 + xl, k * 64:(k + 1) * 64, :] = x[xl * 64:(xl + 1) * 64, xh * 640:(xh + 1) * 640]

    o = a = None
    for h, (tok, og, keep) in enumerate(((tok_ref, og_ref, keep_ref), (tok2_ref, og2_ref, send_ref))):
        cols = pl.ds(h * 512, 512)
        other = pl.ds((1 - h) * 512, 512)
        m1, m2 = r_ref[0:1, cols], r2_ref[0:1, other]
        top = jnp.maximum(m1, m2)
        w1, w2 = jnp.exp(m1 - top), jnp.exp(m2 - top)
        total = w1 * r_ref[1:2, cols] + w2 * r2_ref[1:2, other]
        row = (w1 * r_ref[2:3, cols] + w2 * r2_ref[2:3, other]) / total
        combine = jnp.exp(lg_ref[:, cols] - top) / total
        part = combine * (cg_ref[:, cols] - row)
        keep[0:128, :] = e_ref[:, cols]
        keep[128:256, :] = part
        keep[256:384, :] = dc_ref[:, cols]
        keep[384:392, 0:LANES] = p_ref[...]
        keep[384:392, LANES:512] = jnp.zeros((8, 512 - LANES), F32)
        o1 = nn(combine.astype(BF), og[...])
        a1 = nn(part.astype(BF), tok[...])
        o, a = (o1, a1) if h == 0 else (o + o1, a + a1)
    put(0, o.astype(BF))
    put(1, a.astype(BF))
    put(2, bc_ref[0:128, :])
    put(3, bc_ref[128:256, :])
    stats = stat_rows(p_ref[...])
    for j in range(4):
        out_ref[j, 256:272, :] = stats


def merge_stats(ps, groups, exact=True):
    ms = ps
    ss = [roll(p, -groups) for p in ps]
    ts = [roll(p, -2 * groups) for p in ps]
    lane = lane_of((8, LANES))
    ok = lane < groups
    ms = [jnp.where(ok, v, 0.0) for v in ms]
    ss = [jnp.where(ok, v, 1.0) for v in ss]
    ts = [jnp.where(ok, v, 0.0) for v in ts]
    top = ms[0]
    for v in ms[1:]:
        top = jnp.maximum(top, v)
    if not exact:
        top = sum(v.astype(F32) for v in split(top, 2))
    ws = [jnp.exp(v - top) for v in ms]
    total = sum(w * s for w, s in zip(ws, ss))
    mean = sum(w * s * t for w, s, t in zip(ws, ss, ts)) / total
    if not exact:
        mean = sum(v.astype(F32) for v in split(mean, 2))
    return top, total, mean, ws, [t - mean for t in ts]


def x_kernel(got_ref, out_ref):
    xl = lax.axis_index("xl")
    top, total, mean, ws, ds = merge_stats([stat_read(got_ref[j, 256:272, :]) for j in range(4)], 16, False)
    ws = [columns(w, 8, xl * 8) for w in ws]
    ds = [columns(d, 8, xl * 8) for d in ds]

    def rows(j, k):
        return got_ref[j, k * 64:(k + 1) * 64, :].astype(F32)

    o = sum(rows(j, 0) for j in range(4))
    a = sum(rows(j, 1) for j in range(4))
    cs = [ws[j] * rows(j, 3) for j in range(4)]
    b = sum(ws[j] * rows(j, 2) + ds[j] * cs[j] for j in range(4))
    c = sum(cs)
    lane8 = lane_of((8, LANES))
    ok = lane8 < 16
    p = jnp.where(ok, top, 0.0) + roll(jnp.where(ok, total, 0.0), 16) + roll(jnp.where(ok, mean, 0.0), 32)
    hi, mid = split(p, 2)
    stats = roll(hi.astype(F32), 32) + roll(mid.astype(F32), 80)
    stats = jnp.broadcast_to(stats[None], (8, 8, LANES)).reshape(64, LANES)
    lane = lane_of((64, LANES))
    for k in range(16):
        first = WIDE * k
        j = first // LANES
        cut = (j + 1) * LANES - first
        chunks = []
        for n, x in enumerate((o, a, b, c)):
            v = x[:, j * LANES:(j + 1) * LANES]
            if cut < WIDE:
                v = jnp.where(lane < WIDE - cut, x[:, (j + 1) * LANES:(j + 2) * LANES], v)
            chunks.append(roll(v, WIDE * n - first))
        low = jnp.where(lane < 40, chunks[0], jnp.where(lane < 80, chunks[1], jnp.where(lane < 120, chunks[2], chunks[3])))
        high = jnp.where(lane < 32, chunks[3], stats)
        out_ref[k * 8:(k + 1) * 8, :, 0:LANES] = low.reshape(8, 8, LANES).astype(BF)
        out_ref[k * 8:(k + 1) * 8, :, LANES:2 * LANES] = high.reshape(8, 8, LANES).astype(BF)


def last_kernel(got_ref, g_ref, g2_hbm, keep_ref, keep2_ref, tg_ref, eg_ref, og_ref, g2_ref, sem):
    fetch = pltpu.make_async_copy(g2_hbm, g2_ref, sem)
    fetch.start()
    xl, y, core = lax.axis_index("xl"), lax.axis_index("y"), lax.axis_index("core")
    big = (8, 2, 8, 8, LANES)
    t0 = got_ref[:, :, 0:LANES].astype(F32).reshape(big)
    t1 = got_ref[:, :, LANES:2 * LANES].astype(F32).reshape(1024, LANES)
    p = t1 + roll(t1, -48)
    s = roll(p, -16).reshape(big)
    t = roll(p, -32).reshape(big)
    m = p.reshape(big)
    t1 = t1.reshape(big)
    lane = lane_of((8, LANES))
    ok = (lane >= 32) & (lane < 48)
    m = jnp.where(ok, m, 0.0)
    s = jnp.where(ok, s, 1.0)
    t = jnp.where(ok, t, 0.0)
    top = jnp.max(m, axis=(0, 2))
    w = jnp.exp(m - top[None, :, None])
    ws = w * s
    total = jnp.sum(ws, axis=(0, 2))
    mean = jnp.sum(ws * t, axis=(0, 2)) / total
    dt = t - mean[None, :, None]
    mine = lane == 32 + xl * 8 + y

    def pick(v):
        return jnp.sum(jnp.where(mine, v, 0.0), axis=-1, keepdims=True)

    wm = pick(w)
    wd = wm * pick(dt)
    acc0 = jnp.sum(t0 * jnp.where(lane < 80, 1.0, jnp.where(lane < 120, wm, wd)), axis=(0, 2))
    acc1 = jnp.sum(jnp.where(lane < 32, t1 * wd, 0.0), axis=(0, 2))
    for c in range(2):
        q = acc0[c]
        last = jnp.where(lane < 8, roll(q, -120), roll(acc1[c], 8))
        grad = roll(q, -40) + (roll(q, -80) + last) / pick(total[c])
        eg_ref[c * 8:(c + 1) * 8, :] = grad[:, 0:WIDE]
        og_ref[c * 8:(c + 1) * 8, :] = q[:, 0:WIDE]

    total_grad = None
    for h, (gr, kr) in enumerate(((g_ref, keep_ref), (g2_ref, keep2_ref))):
        second = (core + h) == 1

        def cols(v):
            return columns(jnp.where(second, v[1], v[0]), 16, 32)

        q = kr[384:392, 0:LANES]
        alpha = jnp.exp(columns(q, 16, 0) - cols(top)) / cols(total)
        shift = columns(q, 16, 32) - cols(mean)
        disp = kr[0:128, :] * alpha
        grad = kr[128:256, :] + disp * (kr[256:384, :] + shift)
        left = jnp.concatenate([grad.astype(BF), disp.astype(BF)], axis=0)
        if h == 1:
            fetch.wait()
        x = tn(left, gr[...])
        total_grad = x if h == 0 else total_grad + x
    tg_ref[...] = total_grad.astype(BF)


def call(kernel, outs, *args, scratch=(), flops=0):
    vm = pl.BlockSpec(memory_space=pltpu.VMEM)
    many = isinstance(outs, list)
    return pl.pallas_call(
        kernel,
        out_shape=outs,
        in_specs=[vm] * len(args),
        out_specs=[vm] * len(outs) if many else vm,
        scratch_shapes=list(scratch),
        compiler_params=pltpu.CompilerParams(vmem_limit_bytes=VMEM_BYTES),
    )(*args)


def shape(*dims, dtype=BF):
    return jax.ShapeDtypeStruct(dims, dtype)


def swap(x):
    return lax.ppermute(x, "core", [(0, 1), (1, 0)])


def per_device(tokens, slot_embed, slot_outputs, output_grad, slot_input_grad):
    f32 = jnp.float32
    op = pl.pallas_call(
        pieces_kernel,
        out_shape=shape(128, 8, LANES),
        in_specs=[pl.BlockSpec(memory_space=pl.ANY)] * 3,
        out_specs=pl.BlockSpec(memory_space=pltpu.VMEM),
        scratch_shapes=[pltpu.VMEM((3, 16, WIDE), BF), pltpu.SemaphoreType.DMA((3,))],
        compiler_params=pltpu.CompilerParams(vmem_limit_bytes=60 * 1024 * 1024),
    )(slot_embed, slot_outputs, slot_input_grad)
    op, tok1 = lax.optimization_barrier((op, tokens))
    tok2 = swap(tok1)
    got = lax.all_to_all(op, YZ, 0, 0, tiled=True)
    op = call(widen_kernel, shape(4, 192, 640), got)
    op, og1 = lax.optimization_barrier((op, output_grad))
    og2 = swap(og1)
    got = lax.all_to_all(op, X, 0, 0, tiled=True)
    wide = shape(128, 1024, dtype=f32)
    g, lg, dg, cg, r = call(
        scores_kernel, [shape(256, 1280), wide, wide, wide, shape(8, 1024, dtype=f32)],
        got, tokens, tok2, output_grad, og2, scratch=[pltpu.VMEM((128, 1280), BF)])
    r2 = swap(r)
    e, dc, p, bc = call(
        slots_kernel, [wide, wide, shape(8, LANES, dtype=f32), shape(256, 1280)], lg, dg, tokens, tok2)
    op, keep, send = call(
        tokens_kernel, [shape(4, 272, 640), shape(392, 512, dtype=f32), shape(392, 512, dtype=f32)],
        lg, cg, r, r2, e, dc, p, bc, tokens, tok2, output_grad, og2)
    got = lax.all_to_all(op, X, 0, 0, tiled=True)
    g2, keep2 = swap(g), swap(send)
    op = call(x_kernel, shape(128, 8, 2 * LANES), got)
    got = lax.all_to_all(op, YZ, 0, 0, tiled=True)
    vm = pl.BlockSpec(memory_space=pltpu.VMEM)
    return pl.pallas_call(
        last_kernel,
        out_shape=[shape(512, 1280), shape(16, WIDE, dtype=f32), shape(16, WIDE, dtype=f32)],
        in_specs=[vm, vm, pl.BlockSpec(memory_space=pl.ANY), vm, vm],
        out_specs=[vm] * 3,
        scratch_shapes=[pltpu.VMEM((256, 1280), BF), pltpu.SemaphoreType.DMA],
        compiler_params=pltpu.CompilerParams(vmem_limit_bytes=VMEM_BYTES),
    )(got, g, g2, keep, keep2)


def solution(mesh):
    fine = Mesh(mesh.devices.reshape(2, 8, 2, 8, 2), ("xh", "z", "core", "y", "xl"))
    rows = P(("xh", "z", "core", "y", "xl"), None)
    slot = P(("y", "xl"), ("xh", "z", "core"))
    return jax.shard_map(
        per_device,
        mesh=fine,
        in_specs=(rows, slot, slot, rows, slot),
        out_specs=(rows, slot, slot),
        check_vma=False,
    )
```

```python
import jax
import jax.numpy as jnp
from jax import lax
from jax.experimental import pallas as pl
from jax.experimental.pallas import tpu as pltpu
from jax.sharding import Mesh, PartitionSpec as P

BF = jnp.bfloat16
F32 = jnp.float32
YZ = ("z", "core", "y")
X = ("xh", "xl")
LANES = 128
WIDE = 40
VMEM_BYTES = 16 * 1024 * 1024


def nt(a, b):
    return lax.dot_general(a, b, (((1,), (1,)), ((), ())), preferred_element_type=F32)


def nn(a, b):
    return lax.dot_general(a, b, (((1,), (0,)), ((), ())), preferred_element_type=F32)


def tn(a, b):
    return lax.dot_general(a, b, (((0,), (0,)), ((), ())), preferred_element_type=F32)


def roll(x, shift):
    shift %= LANES
    return x if shift == 0 else pltpu.roll(x, shift, axis=x.ndim - 1)


def lane_of(shape):
    return lax.broadcasted_iota(jnp.int32, shape, len(shape) - 1)


def columns(p, n, first):
    shape = (n, 8, LANES)
    pick = lane_of(shape) == lax.broadcasted_iota(jnp.int32, shape, 0) + first
    x = jnp.where(pick, jnp.broadcast_to(p[None], shape), 0.0)
    return jnp.sum(x, axis=2, keepdims=True).reshape(n * 8, 1)


def packed(v, n, first):
    shape = (n, 8, LANES)
    pick = lane_of(shape) == lax.broadcasted_iota(jnp.int32, shape, 0) + first
    x = jnp.where(pick, jnp.broadcast_to(v.reshape(n, 8, 1), shape), 0.0)
    return jnp.sum(x, axis=0)


def split(x, n):
    parts = []
    for _ in range(n):
        part = x.astype(BF)
        parts.append(part)
        x = x - part.astype(F32)
    return parts


def stat_rows(p):
    a, b, c = split(p, 3)
    rest = jnp.zeros((8, 640 - 3 * LANES), BF)
    top = jnp.concatenate([a, b, c, rest], axis=1).astype(F32)
    return top.astype(BF)


def stat_read(rows):
    f = rows.astype(F32)[:8]
    return f[:, :LANES] + f[:, LANES:2 * LANES] + f[:, 2 * LANES:3 * LANES]


def pieces_kernel(e_ref, o_ref, i_ref, out_ref, in_ref, sems):
    copies = [pltpu.make_async_copy(ref, in_ref.at[k], sems.at[k]) for k, ref in enumerate((e_ref, o_ref, i_ref))]
    for copy in copies:
        copy.start()
    for copy in copies:
        copy.wait()

    def at(k):
        x = in_ref[k].astype(F32)
        x = jnp.concatenate([x, jnp.zeros((16, LANES - WIDE), F32)], axis=1)
        return roll(x, k * WIDE)

    x = at(0) + at(1) + at(2)
    for half in range(2):
        rows = x[half * 8:half * 8 + 8]
        many = jnp.broadcast_to(rows[None], (8, 8, LANES)).astype(BF)
        for z in range(8):
            at_row = (z * 2 + half) * 8
            out_ref[at_row:at_row + 8] = many


def widen_kernel(got_ref, out_ref):
    lane = lane_of((64, LANES))
    blocks = [got_ref[k * 8:(k + 1) * 8].astype(F32).reshape(64, LANES) for k in range(16)]
    for a in range(3):
        tiles = [None] * 5
        for k in range(16):
            x = roll(blocks[k], WIDE * (k - a))
            first, last = WIDE * k, WIDE * k + WIDE
            for j in range(first // LANES, (last - 1) // LANES + 1):
                lo = max(first - j * LANES, 0)
                tiles[j] = x if tiles[j] is None else jnp.where(lane >= lo, x, tiles[j])
        whole = jnp.concatenate(tiles, axis=1).astype(BF)
        for j in range(4):
            out_ref[j, a * 64:(a + 1) * 64, :] = whole


def scores_kernel(got_ref, tok_ref, tok2_ref, og_ref, og2_ref, g_ref, lg_ref, dg_ref, cg_ref, r_ref, outs_ref):
    for xl in range(2):
        for xh in range(2):
            at, cols, j = xl * 64, pl.ds(xh * 640, 640), xh * 2 + xl
            g_ref[at:at + 64, cols] = got_ref[j, 0:64, :]
            outs_ref[at:at + 64, cols] = got_ref[j, 64:128, :]
            g_ref[128 + at:192 + at, cols] = got_ref[j, 128:192, :]
    g = g_ref[...]
    outs = outs_ref[...]
    r_ref[...] = jnp.zeros_like(r_ref)
    for h, (tok, og) in enumerate(((tok_ref, og_ref), (tok2_ref, og2_ref))):
        cols = pl.ds(h * 512, 512)
        both = nt(g, tok[...])
        cgrad = nt(outs, og[...])
        logits = both[:128]
        lg_ref[:, cols] = logits
        dg_ref[:, cols] = both[128:]
        cg_ref[:, cols] = cgrad
        top = jnp.max(logits, axis=0, keepdims=True)
        raised = jnp.exp(logits - top)
        r_ref[0:1, cols] = top
        r_ref[1:2, cols] = jnp.sum(raised, axis=0, keepdims=True)
        r_ref[2:3, cols] = jnp.sum(raised * cgrad, axis=0, keepdims=True)


def slots_kernel(lg_ref, dg_ref, tok_ref, tok2_ref, e_ref, dc_ref, p_ref, bc_ref):
    logits = lg_ref[...]
    dgrad = dg_ref[...]
    m = jnp.max(logits, axis=1, keepdims=True)
    e = jnp.exp(logits - m)
    s = jnp.sum(e, axis=1, keepdims=True)
    t = jnp.sum(e * dgrad, axis=1, keepdims=True) / s
    dc = dgrad - t
    e_ref[...] = e
    dc_ref[...] = dc
    p_ref[...] = packed(m, 16, 0) + packed(s, 16, 16) + packed(t, 16, 32)
    left = jnp.concatenate([(e * dc).astype(BF), e.astype(BF)], axis=0)
    bc_ref[...] = (nn(left[:, :512], tok_ref[...]) + nn(left[:, 512:], tok2_ref[...])).astype(BF)


def tokens_kernel(lg_ref, cg_ref, r_ref, r2_ref, e_ref, dc_ref, p_ref, bc_ref, tok_ref, tok2_ref, og_ref, og2_ref,
                  out_ref, keep_ref, send_ref):
    def put(k, x):
        for xh in range(2):
            for xl in range(2):
                out_ref[xh * 2 + xl, k * 64:(k + 1) * 64, :] = x[xl * 64:(xl + 1) * 64, xh * 640:(xh + 1) * 640]

    o = a = None
    for h, (tok, og, keep) in enumerate(((tok_ref, og_ref, keep_ref), (tok2_ref, og2_ref, send_ref))):
        cols = pl.ds(h * 512, 512)
        other = pl.ds((1 - h) * 512, 512)
        m1, m2 = r_ref[0:1, cols], r2_ref[0:1, other]
        top = jnp.maximum(m1, m2)
        w1, w2 = jnp.exp(m1 - top), jnp.exp(m2 - top)
        total = w1 * r_ref[1:2, cols] + w2 * r2_ref[1:2, other]
        row = (w1 * r_ref[2:3, cols] + w2 * r2_ref[2:3, other]) / total
        combine = jnp.exp(lg_ref[:, cols] - top) / total
        part = combine * (cg_ref[:, cols] - row)
        keep[0:128, :] = e_ref[:, cols]
        keep[128:256, :] = part
        keep[256:384, :] = dc_ref[:, cols]
        keep[384:392, 0:LANES] = p_ref[...]
        keep[384:392, LANES:512] = jnp.zeros((8, 512 - LANES), F32)
        o1 = nn(combine.astype(BF), og[...])
        a1 = nn(part.astype(BF), tok[...])
        o, a = (o1, a1) if h == 0 else (o + o1, a + a1)
    put(0, o.astype(BF))
    put(1, a.astype(BF))
    put(2, bc_ref[0:128, :])
    put(3, bc_ref[128:256, :])
    stats = stat_rows(p_ref[...])
    for j in range(4):
        out_ref[j, 256:264, :] = stats


def merge_stats(ps, groups, exact=True):
    ms = ps
    ss = [roll(p, -groups) for p in ps]
    ts = [roll(p, -2 * groups) for p in ps]
    lane = lane_of((8, LANES))
    ok = lane < groups
    ms = [jnp.where(ok, v, 0.0) for v in ms]
    ss = [jnp.where(ok, v, 1.0) for v in ss]
    ts = [jnp.where(ok, v, 0.0) for v in ts]
    top = ms[0]
    for v in ms[1:]:
        top = jnp.maximum(top, v)
    if not exact:
        top = sum(v.astype(F32) for v in split(top, 2))
    ws = [jnp.exp(v - top) for v in ms]
    total = sum(w * s for w, s in zip(ws, ss))
    mean = sum(w * s * t for w, s, t in zip(ws, ss, ts)) / total
    if not exact:
        mean = sum(v.astype(F32) for v in split(mean, 2))
    return top, total, mean, ws, [t - mean for t in ts]


def x_kernel(got_ref, out_ref):
    xl = lax.axis_index("xl")
    top, total, mean, ws, ds = merge_stats([stat_read(got_ref[j, 256:264, :]) for j in range(4)], 16, False)
    ws = [columns(w, 8, xl * 8) for w in ws]
    ds = [columns(d, 8, xl * 8) for d in ds]

    def rows(j, k):
        return got_ref[j, k * 64:(k + 1) * 64, :].astype(F32)

    o = sum(rows(j, 0) for j in range(4))
    a = sum(rows(j, 1) for j in range(4))
    cs = [ws[j] * rows(j, 3) for j in range(4)]
    b = sum(ws[j] * rows(j, 2) + ds[j] * cs[j] for j in range(4))
    c = sum(cs)
    lane8 = lane_of((8, LANES))
    ok = lane8 < 16
    p = jnp.where(ok, top, 0.0) + roll(jnp.where(ok, total, 0.0), 16) + roll(jnp.where(ok, mean, 0.0), 32)
    hi, mid = split(p, 2)
    stats = roll(hi.astype(F32), 32) + roll(mid.astype(F32), 80)
    stats = jnp.broadcast_to(stats[None], (8, 8, LANES)).reshape(64, LANES)
    lane = lane_of((64, LANES))
    for k in range(16):
        first = WIDE * k
        j = first // LANES
        cut = (j + 1) * LANES - first
        chunks = []
        for n, x in enumerate((o, a, b, c)):
            v = x[:, j * LANES:(j + 1) * LANES]
            if cut < WIDE:
                v = jnp.where(lane < WIDE - cut, x[:, (j + 1) * LANES:(j + 2) * LANES], v)
            chunks.append(roll(v, WIDE * n - first))
        low = jnp.where(lane < 40, chunks[0], jnp.where(lane < 80, chunks[1], jnp.where(lane < 120, chunks[2], chunks[3])))
        high = jnp.where(lane < 32, chunks[3], stats)
        out_ref[k * 8:(k + 1) * 8, :, 0:LANES] = low.reshape(8, 8, LANES).astype(BF)
        out_ref[k * 8:(k + 1) * 8, :, LANES:2 * LANES] = high.reshape(8, 8, LANES).astype(BF)


def last_kernel(got_ref, g_ref, g2_ref, keep_ref, keep2_ref, tg_ref, eg_ref, og_ref):
    xl, y, core = lax.axis_index("xl"), lax.axis_index("y"), lax.axis_index("core")
    big = (8, 2, 8, 8, LANES)
    t0 = got_ref[:, :, 0:LANES].astype(F32).reshape(big)
    t1 = got_ref[:, :, LANES:2 * LANES].astype(F32).reshape(1024, LANES)
    p = t1 + roll(t1, -48)
    s = roll(p, -16).reshape(big)
    t = roll(p, -32).reshape(big)
    m = p.reshape(big)
    t1 = t1.reshape(big)
    lane = lane_of((8, LANES))
    ok = (lane >= 32) & (lane < 48)
    m = jnp.where(ok, m, 0.0)
    s = jnp.where(ok, s, 1.0)
    t = jnp.where(ok, t, 0.0)
    top = jnp.max(m, axis=(0, 2))
    w = jnp.exp(m - top[None, :, None])
    ws = w * s
    total = jnp.sum(ws, axis=(0, 2))
    mean = jnp.sum(ws * t, axis=(0, 2)) / total
    dt = t - mean[None, :, None]
    mine = lane == 32 + xl * 8 + y

    def pick(v):
        return jnp.sum(jnp.where(mine, v, 0.0), axis=-1, keepdims=True)

    wm = pick(w)
    wd = wm * pick(dt)
    acc0 = jnp.sum(t0 * jnp.where(lane < 80, 1.0, jnp.where(lane < 120, wm, wd)), axis=(0, 2))
    acc1 = jnp.sum(jnp.where(lane < 32, t1 * wd, 0.0), axis=(0, 2))
    for c in range(2):
        q = acc0[c]
        last = jnp.where(lane < 8, roll(q, -120), roll(acc1[c], 8))
        grad = roll(q, -40) + (roll(q, -80) + last) / pick(total[c])
        eg_ref[c * 8:(c + 1) * 8, :] = grad[:, 0:WIDE]
        og_ref[c * 8:(c + 1) * 8, :] = q[:, 0:WIDE]

    total_grad = None
    for h, (gr, kr) in enumerate(((g_ref, keep_ref), (g2_ref, keep2_ref))):
        second = (core + h) == 1

        def cols(v):
            return columns(jnp.where(second, v[1], v[0]), 16, 32)

        q = kr[384:392, 0:LANES]
        alpha = jnp.exp(columns(q, 16, 0) - cols(top)) / cols(total)
        shift = columns(q, 16, 32) - cols(mean)
        disp = kr[0:128, :] * alpha
        grad = kr[128:256, :] + disp * (kr[256:384, :] + shift)
        left = jnp.concatenate([grad.astype(BF), disp.astype(BF)], axis=0)
        x = tn(left, gr[...])
        total_grad = x if h == 0 else total_grad + x
    tg_ref[...] = total_grad.astype(BF)


def call(kernel, outs, *args, scratch=(), flops=0):
    vm = pl.BlockSpec(memory_space=pltpu.VMEM)
    many = isinstance(outs, list)
    return pl.pallas_call(
        kernel,
        out_shape=outs,
        in_specs=[vm] * len(args),
        out_specs=[vm] * len(outs) if many else vm,
        scratch_shapes=list(scratch),
        compiler_params=pltpu.CompilerParams(vmem_limit_bytes=VMEM_BYTES),
    )(*args)


def shape(*dims, dtype=BF):
    return jax.ShapeDtypeStruct(dims, dtype)


def swap(x):
    return lax.ppermute(x, "core", [(0, 1), (1, 0)])


def per_device(tokens, slot_embed, slot_outputs, output_grad, slot_input_grad):
    f32 = jnp.float32
    op = pl.pallas_call(
        pieces_kernel,
        out_shape=shape(128, 8, LANES),
        in_specs=[pl.BlockSpec(memory_space=pl.ANY)] * 3,
        out_specs=pl.BlockSpec(memory_space=pltpu.VMEM),
        scratch_shapes=[pltpu.VMEM((3, 16, WIDE), BF), pltpu.SemaphoreType.DMA((3,))],
        compiler_params=pltpu.CompilerParams(vmem_limit_bytes=60 * 1024 * 1024),
    )(slot_embed, slot_outputs, slot_input_grad)
    op, tok1 = lax.optimization_barrier((op, tokens))
    tok2 = swap(tok1)
    got = lax.all_to_all(op, YZ, 0, 0, tiled=True)
    op = call(widen_kernel, shape(4, 192, 640), got)
    op, og1 = lax.optimization_barrier((op, output_grad))
    og2 = swap(og1)
    got = lax.all_to_all(op, X, 0, 0, tiled=True)
    wide = shape(128, 1024, dtype=f32)
    g, lg, dg, cg, r = call(
        scores_kernel, [shape(256, 1280), wide, wide, wide, shape(8, 1024, dtype=f32)],
        got, tokens, tok2, output_grad, og2, scratch=[pltpu.VMEM((128, 1280), BF)])
    r2 = swap(r)
    e, dc, p, bc = call(
        slots_kernel, [wide, wide, shape(8, LANES, dtype=f32), shape(256, 1280)], lg, dg, tokens, tok2)
    op, keep, send = call(
        tokens_kernel, [shape(4, 264, 640), shape(392, 512, dtype=f32), shape(392, 512, dtype=f32)],
        lg, cg, r, r2, e, dc, p, bc, tokens, tok2, output_grad, og2)
    got = lax.all_to_all(op, X, 0, 0, tiled=True)
    g2, keep2 = swap(g), swap(send)
    op = call(x_kernel, shape(128, 8, 2 * LANES), got)
    got = lax.all_to_all(op, YZ, 0, 0, tiled=True)
    return call(
        last_kernel,
        [shape(512, 1280), shape(16, WIDE, dtype=f32), shape(16, WIDE, dtype=f32)],
        got, g, g2, keep, keep2)


def solution(mesh):
    fine = Mesh(mesh.devices.reshape(2, 8, 2, 8, 2), ("xh", "z", "core", "y", "xl"))
    rows = P(("xh", "z", "core", "y", "xl"), None)
    slot = P(("y", "xl"), ("xh", "z", "core"))
    return jax.shard_map(
        per_device,
        mesh=fine,
        in_specs=(rows, slot, slot, rows, slot),
        out_specs=(rows, slot, slot),
        check_vma=False,
    )
```
